32 devices in a mesh: grp: 2 (over x), ang: 2 (over core), zs: 8 (over z, y).
Axes of the slice: x: 2, y: 2, z: 4, core: 2. Of those that a mesh axis runs over, the one named last changes fastest.
Arguments:
- projections: bfloat16 [256, 256, 4096], P(('grp', 'ang', 'zs')), parts along dimension 0, may hold values from 0 to 6
- view_angle: float32 [256], P(('grp', 'ang', 'zs')), parts along dimension 0, may hold values from 0 to 4.14
- band_offset: int32 [256, 8], P(('grp', 'ang', 'zs')), parts along dimension 0, may hold values from 0 to 224
- band_count: int32 [256, 8], P(('grp', 'ang', 'zs')), parts along dimension 0, may hold values from 0 to 32, as said below
- fp_start: int32 [256], P(('grp', 'ang', 'zs')), parts along dimension 0, may hold values from 0 to 3072
- footprint: bfloat16 [256, 1024, 128], P(('grp', 'ang')), parts along dimension 0, may hold values from -0.75 to 0.75
Outputs:
- volume: float32 [512, 128], P(('grp', 'zs'), 'ang'), parts along dimension 0
The draws below stay inside these ranges and needn't reach their ends.
There are 2 independent parts, one for each index of `grp`. The reference program is written for one: setup_inputs(seed, part) draws one part's arguments, and reference() takes and returns one part's arrays. A program takes and returns all parts, laid end to end along the dimension named above; each array names one. Nothing has to cross between parts.
Inputs may be any that keep to these rules, and one draw needn't show every extreme that they name: `band_count`: counts reach 32 in every draw.
All inputs are finite; a program needn't handle non-finite values.
Results may differ from the reference program's by a relative error of at most 0.00035.
The reference program's roundings to bfloat16 on the way count: a program that leaves them out, or rounds other values in their place, can miss the bound.
Values may be sent and summed in bfloat16 or wider, within the bound.
A program may use at most 192 MiB of HBM per device.

```python
import math
import jax
import jax.numpy as jnp
from jax import lax

DW = 4096
FB = 1024
DR = 256
BAND = 32
VX = 128
ANGLES = 128
NZ = 256
N_ZS = 8


def draw_band_count(key, part):
    key = jax.random.fold_in(key, 7)
    counts = jax.random.randint(key, (ANGLES, N_ZS), 0, BAND + 1)
    return counts.at[0, 0].set(BAND).astype(jnp.int32)


def line_integrals(key, level_low, level_high, texture):
    level_key, rough_key = jax.random.split(key)
    column_pos = jnp.arange(DW).astype(jnp.float32)
    across = (2.0 * column_pos + 1.0) / DW - 1.0
    profile = jnp.sqrt(1.0 - 0.8 * across * across)
    level = jax.random.uniform(level_key, (ANGLES, DR, 1), jnp.float32, level_low, level_high)
    return level * profile[None, None, :] + texture(rough_key)


def draw_projections(key, part):
    key = jax.random.fold_in(key, 11)
    values = line_integrals(key, 1.0, 2.5, lambda rough_key: 0.35 * jax.random.normal(rough_key, (ANGLES, DR, DW), jnp.float32))
    return jnp.clip(values, 0.0, 6.0).astype(jnp.bfloat16)


def plant(values, stream_key, least, largest):
    place = [jax.random.randint(jax.random.fold_in(stream_key, axis), (), 0, length) for axis, length in enumerate(values.shape)]
    widest = values.shape.index(max(values.shape))
    neighbour = place[:widest] + [(place[widest] + 1) % values.shape[widest]] + place[widest + 1:]
    return values.at[tuple(place)].set(least).at[tuple(neighbour)].set(largest)


def level_of(rng, extent, cuts, smallest, top_value):
    gain, own = 1.0, jax.random.fold_in(rng, 6)
    for axis_at, shards_of in cuts:
        draws = jnp.exp(jax.random.uniform(jax.random.fold_in(own, axis_at), (shards_of,), jnp.float32, smallest / len(cuts), top_value / len(cuts)))
        gain = gain * jnp.repeat(draws, extent[axis_at] // shards_of).reshape([-1 if axis == axis_at else 1 for axis in range(len(extent))])
    return gain


def centred(rng, dims, scale, limit, cuts=(), dtype=jnp.bfloat16):
    result = jax.random.normal(rng, dims, jnp.float32) * scale
    if len(cuts) > 0:
        result = level_of(rng, dims, cuts, -0.22, 0.18) * result
    return jnp.clip(result, min=-limit, max=limit).astype(dtype)


def setup_inputs(seed: int = 0, part: int = 0) -> dict:
    streams_of = jax.random.split(jax.random.key(seed), 7)
    part_keys = jax.random.split(jax.random.fold_in(streams_of[6], part), 7)
    projections = draw_projections(jax.random.fold_in(jax.random.fold_in(streams_of[6], part), 71), part)
    view_angle = jnp.clip(4.14 * jax.random.uniform(part_keys[1], (ANGLES,), jnp.float32) ** level_of(part_keys[1], (ANGLES,), ((0, 16),), -0.2, 0.2), 0.0, 4.14)
    band_offset = plant(jax.random.randint(part_keys[2], (ANGLES, N_ZS), 0, DR - BAND + 1), jax.random.fold_in(part_keys[2], 1), 0, DR - BAND).astype(jnp.int32)
    band_count = draw_band_count(jax.random.fold_in(jax.random.fold_in(streams_of[6], part), 71), part)
    fp_start = plant(jax.random.randint(part_keys[4], (ANGLES,), 0, DW - FB + 1), jax.random.fold_in(part_keys[4], 1), 0, DW - FB).astype(jnp.int32)
    footprint = centred(part_keys[5], (ANGLES, FB, VX), (ANGLES * FB // 2048 + 1) ** -0.5, 0.75, ((0, 2),))
    return {"projections": projections, "view_angle": view_angle, "band_offset": band_offset, "band_count": band_count, "fp_start": fp_start, "footprint": footprint}


fan_half = 0.5


def parker_weight(beta, columns):
    column_pos = jnp.arange(columns).astype(jnp.float32)
    gamma = fan_half * ((2.0 * column_pos + 1.0) / columns - 1.0)
    rising = jnp.sin(math.pi / 4.0 * beta / (fan_half - gamma)) ** 2
    falling = jnp.sin(math.pi / 4.0 * (math.pi + 2.0 * fan_half - beta) / (fan_half + gamma)) ** 2
    parker = jnp.where(beta < 2.0 * (fan_half - gamma), rising, jnp.where(beta > math.pi - 2.0 * gamma, falling, 1.0))
    return parker * jnp.cos(gamma)


def ramp_table(first_col, columns, width):
    offsets = jnp.arange(columns).astype(jnp.int32)[:, None] - first_col.astype(jnp.int32) - jnp.arange(width).astype(jnp.int32)[None, :]
    offset_real = offsets.astype(jnp.float32)
    is_odd = (jnp.abs(offsets) % 2) == 1
    values = jnp.where(offsets == 0, 0.25, jnp.where(is_odd, -1.0 / (math.pi ** 2 * jnp.maximum(offset_real * offset_real, 1.0)), 0.0))
    return values.astype(jnp.bfloat16)


def filter_view(packed):
    view_rows, beta, first_col = packed
    weight = parker_weight(beta, DW)
    weighted = (view_rows.astype(jnp.float32) * weight[None, :]).astype(jnp.bfloat16)
    kernel = ramp_table(first_col, DW, FB)
    return jnp.dot(weighted.astype(jnp.float32), kernel.astype(jnp.float32)).astype(jnp.bfloat16)


def cut_band(view_filtered, first_row, row_count):
    rows_taken = lax.dynamic_slice_in_dim(view_filtered, first_row.astype(jnp.int32), BAND, 0)
    keep_rows = jnp.arange(BAND).astype(jnp.int32) < row_count.astype(jnp.int32)
    return jnp.where(keep_rows[:, None], rows_taken, jnp.zeros_like(rows_taken))


def reference(projections, view_angle, band_offset, band_count, fp_start, footprint):
    filtered = lax.map(filter_view, (projections, view_angle, fp_start))
    bands = jax.vmap(jax.vmap(cut_band, in_axes=(None, 0, 0)), in_axes=(0, 0, 0))(filtered, band_offset, band_count)
    slabs = jnp.einsum("aspc,acv->spv", bands.astype(jnp.float32), footprint.astype(jnp.float32))
    return slabs.reshape(NZ, VX)
```

```python
import functools
import math

import jax
import jax.numpy as jnp
from jax import lax
from jax.experimental import pallas as pl
from jax.experimental.pallas import tpu as pltpu
from jax.sharding import PartitionSpec as P

BAND = 32
FAN_HALF = 0.5
LANES = 128
ALIGN = 32
KC = 512
F32 = jnp.float32
BF16 = jnp.bfloat16
NT = (((1,), (1,)), ((), ()))
TN = (((0,), (0,)), ((), ()))


def fan_weight(beta, columns):
    shape = (beta.shape[0], columns)
    position = lax.broadcasted_iota(jnp.int32, shape, 1).astype(F32)
    gamma = FAN_HALF * ((2.0 * position + 1.0) / columns - 1.0)
    rising = math.pi / 4.0 * beta / (FAN_HALF - gamma)
    falling = math.pi / 4.0 * (math.pi + 2.0 * FAN_HALF - beta) / (FAN_HALF + gamma)
    flat = jnp.full(shape, math.pi / 2.0, F32)
    angle = jnp.where(
        beta < 2.0 * (FAN_HALF - gamma),
        rising,
        jnp.where(beta > math.pi - 2.0 * gamma, falling, flat),
    )
    return jnp.sin(angle) ** 2 * jnp.cos(gamma)


def odd_ramp(offsets):
    real = offsets.astype(F32)
    return (-1.0 / (math.pi**2 * (real * real))).astype(BF16)


def kernel(
    sizes,
    start_ref, offset_ref, count_ref, angle_ref, proj_ref, foot_ref, out_ref,
    proj_buf, foot_buf, foot_wide, weight, pick, ramp_even, ramp_odd,
    w_even, w_odd, diag_even, diag_odd, grid_rows, volume, proj_sem, foot_sem,
):
    n_zs, n_ang, views, columns, width = sizes
    half = columns // 2
    window = (width + ALIGN) // 2
    my_zs = lax.axis_index("zs")

    def proj_copy(view, slot):
        return pltpu.make_async_copy(proj_ref.at[view], proj_buf.at[slot], proj_sem.at[slot])

    proj_copy(0, 0).start()
    proj_copy(1, 1).start()
    foot_copy = pltpu.make_async_copy(
        foot_ref.at[pl.ds(my_zs * views, views)], foot_buf, foot_sem
    )
    foot_copy.start()

    weight[...] = fan_weight(angle_ref[...], columns)

    row = lax.broadcasted_iota(jnp.int32, (256, 256), 0)
    col = lax.broadcasted_iota(jnp.int32, (256, 256), 1)
    source = jnp.where(col < LANES, 2 * col, 2 * (col - LANES) + 1)
    pick[...] = jnp.where(row == source, 1.0, 0.0).astype(BF16)

    ramp_rows = ramp_even.shape[0]
    block = 128
    shift = half - LANES

    def fill(step, _):
        first = pl.multiple_of(step * block, block)
        row = lax.broadcasted_iota(jnp.int32, (block, LANES), 0) + first
        lane = lax.broadcasted_iota(jnp.int32, (block, LANES), 1)
        twice = 2 * (lane - row + shift)
        ramp_even[pl.ds(first, block), :] = odd_ramp(twice + 1)
        ramp_odd[pl.ds(first, block), :] = odd_ramp(twice - 1)
        return 0

    lax.fori_loop(0, ramp_rows // block, fill, 0)
    volume[...] = jnp.zeros_like(volume)
    foot_wide[...] = jnp.zeros_like(foot_wide)
    for part in (w_even, w_odd):
        part[:, half:] = jnp.zeros((part.shape[0], part.shape[1] - half), BF16)
    foot_copy.wait()

    def view_step(view, _):
        slot = lax.rem(view, 2)
        proj_copy(view, slot).wait()
        for j in range(columns // 256):
            cols = pl.ds(256 * j, 256)
            scaled = (
                proj_buf[slot, :, cols].astype(F32) * weight[pl.ds(view, 1), cols]
            ).astype(BF16)
            parted = jnp.dot(scaled, pick[...], preferred_element_type=F32).astype(BF16)
            w_even[:, pl.ds(LANES * j, LANES)] = parted[:, :LANES]
            w_odd[:, pl.ds(LANES * j, LANES)] = parted[:, LANES:]

        @pl.when(view + 2 < views)
        def _():
            proj_copy(view + 2, slot).start()

        first = start_ref[view]
        base = first // ALIGN
        lead = first - base * ALIGN
        row0 = base * (ALIGN // 2)
        tile = row0 // LANES
        inner = pl.multiple_of(row0 - tile * LANES, 16)
        row0 = pl.multiple_of(row0, 16)
        for part, diag in ((w_even, diag_even), (w_odd, diag_odd)):
            near = part[:, pl.ds(pl.multiple_of(tile * LANES, LANES), diag.shape[0])]
            diag[...] = 0.25 * near.astype(F32).T

        foot_wide[pl.ds(ALIGN, width), :] = foot_buf[view].astype(F32)
        total = None
        for parity, ramp, part, diag in (
            (0, ramp_even, w_odd, diag_even),
            (1, ramp_odd, w_even, diag_odd),
        ):
            acc = diag[pl.ds(inner, window), :]
            for kc in range(half // KC):
                lhs = jnp.concatenate(
                    [
                        ramp[pl.ds(row0 + (shift - KC * kc - LANES * j), window), :]
                        for j in range(KC // LANES)
                    ],
                    axis=1,
                )
                acc += lax.dot_general(
                    lhs, part[:, KC * kc : KC * kc + KC], NT, preferred_element_type=F32
                )
            filtered = acc.astype(BF16)
            foot = foot_wide[pl.ds(ALIGN + parity - lead, window, stride=2), :].astype(BF16)
            term = lax.dot_general(foot, filtered, TN, preferred_element_type=F32)
            total = term if total is None else total + term
        grid_rows[...] = total.T

        place = lax.broadcasted_iota(jnp.int32, (BAND, total.shape[0]), 0)
        for s in range(n_zs):
            rows = grid_rows[pl.ds(offset_ref[view, s], BAND), :]
            volume[s] += jnp.where(place < count_ref[view, s], rows, 0.0)
        return 0

    lax.fori_loop(0, views, view_step, 0)

    share = volume.shape[2] // n_ang
    for s in range(n_zs):
        slab = volume[s]
        for g in range(n_ang):
            piece = slab[:, share * g : share * (g + 1)]
            out_ref[s, g] = jnp.concatenate([piece[: BAND // 2], piece[BAND // 2 :]], axis=1)


def exchange(n_zs, n_ang, send_buf, out_ref, recv_buf, send_sem, recv_sem):
    peers = n_zs * n_ang
    share = out_ref.shape[1]
    my_zs, my_ang = lax.axis_index("zs"), lax.axis_index("ang")
    me = my_zs * n_ang + my_ang
    barrier = pltpu.get_barrier_semaphore()
    for k in range(1, peers):
        peer = lax.rem(me + k, peers)
        pl.semaphore_signal(
            barrier, inc=1,
            device_id={"zs": peer // n_ang, "ang": lax.rem(peer, n_ang)},
            device_id_type=pl.DeviceIdType.MESH,
        )

    pl.semaphore_wait(barrier, peers - 1)
    copies = []
    for k in range(1, peers):
        peer = lax.rem(me + k, peers)
        peer_zs, peer_ang = peer // n_ang, lax.rem(peer, n_ang)
        copy = pltpu.make_async_remote_copy(
            src_ref=send_buf.at[peer_zs, peer_ang],
            dst_ref=recv_buf.at[k],
            send_sem=send_sem.at[k],
            recv_sem=recv_sem.at[k],
            device_id={"zs": peer_zs, "ang": peer_ang},
            device_id_type=pl.DeviceIdType.MESH,
        )
        copy.start()
        copies.append(copy)
    result = send_buf[my_zs, my_ang]
    for k, copy in enumerate(copies):
        copy.wait_recv()
        result += recv_buf[k + 1]
    out_ref[...] = jnp.concatenate([result[:, :share], result[:, share:]], axis=0)
    for copy in copies:
        copy.wait_send()


def shards(n_zs, n_ang, projections, view_angle, band_offset, band_count, fp_start, footprint):
    views, rows, columns = projections.shape
    width, voxels = footprint.shape[1:]
    half = columns // 2
    window = (width + ALIGN) // 2
    ramp_rows = (columns - width) // 2 + (half - LANES) + window
    ramp_rows = -(-ramp_rows // LANES) * LANES
    near = -(-(window + LANES - 16) // LANES) * LANES
    pad = near - width // 2
    peers = n_zs * n_ang
    smem = pl.BlockSpec(memory_space=pltpu.SMEM)
    vmem = pl.BlockSpec(memory_space=pltpu.VMEM)
    hbm = pl.BlockSpec(memory_space=pl.ANY)
    flops = 2 * views * rows * (columns * width // 2 + columns * 256 + width * voxels)
    partial = pl.pallas_call(
        functools.partial(kernel, (n_zs, n_ang, views, columns, width)),
        out_shape=jax.ShapeDtypeStruct((n_zs, n_ang, BAND // 2, voxels), F32),
        in_specs=[smem, smem, smem, vmem, hbm, hbm],
        out_specs=vmem,
        scratch_shapes=[
            pltpu.VMEM((2, rows, columns), BF16),
            pltpu.VMEM((views, width, voxels), BF16),
            pltpu.VMEM((width + 2 * ALIGN, voxels), F32),
            pltpu.VMEM((views, columns), F32),
            pltpu.VMEM((256, 256), BF16),
            pltpu.VMEM((ramp_rows, LANES), BF16),
            pltpu.VMEM((ramp_rows, LANES), BF16),
            pltpu.VMEM((rows, half + pad), BF16),
            pltpu.VMEM((rows, half + pad), BF16),
            pltpu.VMEM((near, rows), F32),
            pltpu.VMEM((near, rows), F32),
            pltpu.VMEM((rows, voxels), F32),
            pltpu.VMEM((n_zs, BAND, voxels), F32),
            pltpu.SemaphoreType.DMA((2,)),
            pltpu.SemaphoreType.DMA,
        ],
        compiler_params=pltpu.CompilerParams(vmem_limit_bytes=48 * 2**20),
        cost_estimate=pl.CostEstimate(
            flops=flops, bytes_accessed=projections.size * 2, transcendentals=0
        ),
        name="filter_backproject",
    )(fp_start, band_offset, band_count, view_angle[:, None], projections, footprint)
    return pl.pallas_call(
        functools.partial(exchange, n_zs, n_ang),
        out_shape=jax.ShapeDtypeStruct((BAND, voxels // n_ang), F32),
        in_specs=[vmem],
        out_specs=vmem,
        scratch_shapes=[
            pltpu.VMEM((peers, BAND // 2, voxels), F32),
            pltpu.SemaphoreType.DMA((peers,)),
            pltpu.SemaphoreType.DMA((peers,)),
        ],
        compiler_params=pltpu.CompilerParams(collective_id=0, has_side_effects=True),
        name="sum_slabs",
    )(partial)


def solution(mesh):
    in_specs = (
        P(("grp", "ang", "zs"), None, None),
        P(("grp", "ang", "zs")),
        P(("grp", "ang", "zs"), None),
        P(("grp", "ang", "zs"), None),
        P(("grp", "ang", "zs")),
        P(("grp", "ang"), None, None),
    )
    out_specs = P(("grp", "zs"), "ang")
    body = functools.partial(shards, mesh.shape["zs"], mesh.shape["ang"])
    return jax.shard_map(body, mesh=mesh, in_specs=in_specs, out_specs=out_specs, check_vma=False)
```

```python
import functools
import math

import jax
import jax.numpy as jnp
from jax import lax
from jax.experimental import pallas as pl
from jax.experimental.pallas import tpu as pltpu
from jax.sharding import PartitionSpec as P

BAND = 32
FAN_HALF = 0.5
LANES = 128
ALIGN = 32
KC = 2048
F32 = jnp.float32
BF16 = jnp.bfloat16
NT = (((1,), (1,)), ((), ()))
TN = (((0,), (0,)), ((), ()))


def fan_weight(beta, columns):
    shape = (beta.shape[0], columns)
    position = lax.broadcasted_iota(jnp.int32, shape, 1).astype(F32)
    gamma = FAN_HALF * ((2.0 * position + 1.0) / columns - 1.0)
    rising = math.pi / 4.0 * beta / (FAN_HALF - gamma)
    falling = math.pi / 4.0 * (math.pi + 2.0 * FAN_HALF - beta) / (FAN_HALF + gamma)
    flat = jnp.full(shape, math.pi / 2.0, F32)
    angle = jnp.where(
        beta < 2.0 * (FAN_HALF - gamma),
        rising,
        jnp.where(beta > math.pi - 2.0 * gamma, falling, flat),
    )
    return jnp.sin(angle) ** 2 * jnp.cos(gamma)


def odd_ramp(offsets):
    real = offsets.astype(F32)
    return (-1.0 / (math.pi**2 * (real * real))).astype(BF16)


def kernel(
    sizes,
    start_hbm, offset_hbm, count_hbm, angle_hbm, proj_ref, foot_ref, out_ref,
    start_ref, offset_ref, count_ref, angle_ref,
    proj_buf, foot_buf, foot_wide, weight, pick, ramp_even, ramp_odd,
    w_even_0, w_odd_0, w_even_1, w_odd_1, diag_even, diag_odd, grid_rows, volume, proj_sem, foot_sem, small_sem,
):
    n_zs, n_ang, views, columns, width = sizes
    half = columns // 2
    window = (width + ALIGN) // 2
    my_zs = lax.axis_index("zs")

    def proj_copy(view, slot):
        return pltpu.make_async_copy(proj_ref.at[view], proj_buf.at[slot], proj_sem.at[slot])

    small = [
        pltpu.make_async_copy(source, target, small_sem.at[i])
        for i, (source, target) in enumerate(
            ((angle_hbm, angle_ref), (start_hbm, start_ref),
             (offset_hbm, offset_ref), (count_hbm, count_ref))
        )
    ]
    for copy in small:
        copy.start()
    proj_copy(0, 0).start()
    proj_copy(1, 1).start()
    foot_copy = pltpu.make_async_copy(
        foot_ref.at[pl.ds(my_zs * views, views)], foot_buf, foot_sem
    )
    foot_copy.start()

    row = lax.broadcasted_iota(jnp.int32, (256, 256), 0)
    col = lax.broadcasted_iota(jnp.int32, (256, 256), 1)
    source = jnp.where(col < LANES, 2 * col, 2 * (col - LANES) + 1)
    pick[...] = jnp.where(row == source, 1.0, 0.0).astype(BF16)

    ramp_rows = ramp_even.shape[0]
    block = 128
    shift = half - LANES

    def fill(step, _):
        first = pl.multiple_of(step * block, block)
        row = lax.broadcasted_iota(jnp.int32, (block, LANES), 0) + first
        lane = lax.broadcasted_iota(jnp.int32, (block, LANES), 1)
        twice = 2 * (lane - row + shift)
        ramp_even[pl.ds(first, block), :] = odd_ramp(twice + 1)
        ramp_odd[pl.ds(first, block), :] = odd_ramp(twice - 1)
        return 0

    lax.fori_loop(0, ramp_rows // block, fill, 0)
    volume[...] = jnp.zeros_like(volume)
    foot_wide[...] = jnp.zeros_like(foot_wide)
    for part in (w_even_0, w_odd_0, w_even_1, w_odd_1):
        part[:, half:] = jnp.zeros((part.shape[0], part.shape[1] - half), BF16)
    for copy in small:
        copy.wait()
    which = lax.broadcasted_iota(jnp.int32, (views, 1), 0)
    beta = jnp.zeros((views, 1), F32)
    for a in range(views):
        beta = jnp.where(which == a, angle_ref[a], beta)
    weight[...] = fan_weight(beta, columns)
    foot_copy.wait()

    def part_block(view, slot, j, w_even, w_odd):
        cols = pl.ds(256 * j, 256)
        scaled = (
            proj_buf[slot, :, cols].astype(F32) * weight[pl.ds(view, 1), cols]
        ).astype(BF16)
        parted = jnp.dot(scaled, pick[...], preferred_element_type=F32).astype(BF16)
        w_even[:, pl.ds(LANES * j, LANES)] = parted[:, :LANES]
        w_odd[:, pl.ds(LANES * j, LANES)] = parted[:, LANES:]

    def view_step(view, now, later):
        following = jnp.minimum(view + 1, views - 1)
        blocks = columns // 256
        chunks = 2 * (half // KC)
        emitted = 0

        first = start_ref[view]
        base = first // ALIGN
        lead = first - base * ALIGN
        row0 = base * (ALIGN // 2)
        tile = row0 // LANES
        inner = pl.multiple_of(row0 - tile * LANES, 16)
        row0 = pl.multiple_of(row0, 16)
        w_even, w_odd = now
        for part, diag in ((w_even, diag_even), (w_odd, diag_odd)):
            near = part[:, pl.ds(pl.multiple_of(tile * LANES, LANES), diag.shape[0])]
            diag[...] = 0.25 * near.astype(F32).T

        foot_wide[pl.ds(ALIGN, width), :] = foot_buf[view].astype(F32)
        total = None
        for parity, ramp, part, diag in (
            (0, ramp_even, w_odd, diag_even),
            (1, ramp_odd, w_even, diag_odd),
        ):
            acc = diag[pl.ds(inner, window), :]
            for kc in range(half // KC):
                lhs = jnp.concatenate(
                    [
                        ramp[pl.ds(row0 + (shift - KC * kc - LANES * j), window), :]
                        for j in range(KC // LANES)
                    ],
                    axis=1,
                )
                acc += lax.dot_general(
                    lhs, part[:, KC * kc : KC * kc + KC], NT, preferred_element_type=F32
                )
                for j in range(blocks // chunks):
                    part_block(following, (now_slot[0] + 1) % 2, emitted, *later)
                    emitted += 1
            filtered = acc.astype(BF16)
            foot = foot_wide[pl.ds(ALIGN + parity - lead, window, stride=2), :].astype(BF16)
            term = lax.dot_general(foot, filtered, TN, preferred_element_type=F32)
            total = term if total is None else total + term
        grid_rows[...] = total.T

        place = lax.broadcasted_iota(jnp.int32, (BAND, total.shape[0]), 0)
        for s in range(n_zs):
            rows = grid_rows[pl.ds(offset_ref[view, s], BAND), :]
            volume[s] += jnp.where(place < count_ref[view, s], rows, 0.0)

    now_slot = [0]
    ring = ((w_even_0, w_odd_0), (w_even_1, w_odd_1))
    proj_copy(0, 0).wait()
    for j in range(columns // 256):
        part_block(0, 0, j, *ring[0])

    @pl.when(2 < views)
    def _():
        proj_copy(2, 0).start()

    def pair_step(pair, _):
        for slot in range(2):
            view = 2 * pair + slot
            other = 1 - slot

            @pl.when(view + 1 < views)
            def _():
                proj_copy(view + 1, other).wait()

            now_slot[0] = slot
            view_step(view, ring[slot], ring[other])

            @pl.when(view + 3 < views)
            def _():
                proj_copy(view + 3, other).start()
        return 0

    lax.fori_loop(0, views // 2, pair_step, 0)

    share = volume.shape[2] // n_ang
    for s in range(n_zs):
        slab = volume[s]
        for g in range(n_ang):
            piece = slab[:, share * g : share * (g + 1)]
            out_ref[g, s] = jnp.concatenate([piece[: BAND // 2], piece[BAND // 2 :]], axis=1)


def greet(peers):
    barrier = pltpu.get_barrier_semaphore()
    for peer in peers:
        pl.semaphore_signal(
            barrier, inc=1, device_id=peer, device_id_type=pl.DeviceIdType.MESH
        )
    return barrier


def partners(n_zs, n_ang):
    my_zs, my_ang = lax.axis_index("zs"), lax.axis_index("ang")
    near = [lax.rem(my_ang + k, n_ang) for k in range(1, n_ang)]
    far = [lax.rem(my_zs + k, n_zs) for k in range(1, n_zs)]
    ids = [{"zs": my_zs, "ang": g} for g in near] + [{"zs": z, "ang": my_ang} for z in far]
    return near, far, ids


def finish(n_zs, n_ang, barrier, send_buf, out_ref, near_buf, sum_buf, far_buf, send_sem, recv_sem):
    share = out_ref.shape[1]
    my_zs, my_ang = lax.axis_index("zs"), lax.axis_index("ang")
    near, far, ids = partners(n_zs, n_ang)
    pl.semaphore_wait(barrier, len(ids))

    def start(i, source, target):
        copy = pltpu.make_async_remote_copy(
            src_ref=source, dst_ref=target,
            send_sem=send_sem.at[i], recv_sem=recv_sem.at[i],
            device_id=ids[i], device_id_type=pl.DeviceIdType.MESH,
        )
        copy.start()
        return copy

    copies = [start(i, send_buf.at[g], near_buf.at[i]) for i, g in enumerate(near)]
    total = send_buf[my_ang]
    for i, copy in enumerate(copies):
        copy.wait_recv()
        total += near_buf[i]
    sum_buf[...] = total
    for i, z in enumerate(far):
        copies.append(start(len(near) + i, sum_buf.at[z], far_buf.at[i]))
    result = sum_buf[my_zs]
    for i, copy in enumerate(copies[len(near):]):
        copy.wait_recv()
        result += far_buf[i]
    out_ref[...] = jnp.concatenate([result[:, :share], result[:, share:]], axis=0)
    for copy in copies:
        copy.wait_send()


def exchange(n_zs, n_ang, send_buf, out_ref, *scratch):
    barrier = greet(partners(n_zs, n_ang)[2])
    finish(n_zs, n_ang, barrier, send_buf, out_ref, *scratch)


def shards(n_zs, n_ang, projections, view_angle, band_offset, band_count, fp_start, footprint):
    views, rows, columns = projections.shape
    width, voxels = footprint.shape[1:]
    half = columns // 2
    window = (width + ALIGN) // 2
    ramp_rows = (columns - width) // 2 + (half - LANES) + window
    ramp_rows = -(-ramp_rows // LANES) * LANES
    near = -(-(window + LANES - 16) // LANES) * LANES
    pad = near - width // 2
    peers = n_zs + n_ang - 2
    vmem = pl.BlockSpec(memory_space=pltpu.VMEM)
    hbm = pl.BlockSpec(memory_space=pl.ANY)
    flops = 2 * views * rows * (columns * width // 2 + columns * 256 + width * voxels)
    partial = pl.pallas_call(
        functools.partial(kernel, (n_zs, n_ang, views, columns, width)),
        out_shape=jax.ShapeDtypeStruct((n_ang, n_zs, BAND // 2, voxels), F32),
        in_specs=[hbm] * 6,
        out_specs=vmem,
        scratch_shapes=[
            pltpu.SMEM(fp_start.shape, jnp.int32),
            pltpu.SMEM(band_offset.shape, jnp.int32),
            pltpu.SMEM(band_count.shape, jnp.int32),
            pltpu.SMEM(view_angle.shape, F32),
            pltpu.VMEM((2, rows, columns), BF16),
            pltpu.VMEM((views, width, voxels), BF16),
            pltpu.VMEM((width + 2 * ALIGN, voxels), F32),
            pltpu.VMEM((views, columns), F32),
            pltpu.VMEM((256, 256), BF16),
            pltpu.VMEM((ramp_rows, LANES), BF16),
            pltpu.VMEM((ramp_rows, LANES), BF16),
            pltpu.VMEM((rows, half + pad), BF16),
            pltpu.VMEM((rows, half + pad), BF16),
            pltpu.VMEM((rows, half + pad), BF16),
            pltpu.VMEM((rows, half + pad), BF16),
            pltpu.VMEM((near, rows), F32),
            pltpu.VMEM((near, rows), F32),
            pltpu.VMEM((rows, voxels), F32),
            pltpu.VMEM((n_zs, BAND, voxels), F32),
            pltpu.SemaphoreType.DMA((2,)),
            pltpu.SemaphoreType.DMA,
            pltpu.SemaphoreType.DMA((4,)),
        ],
        compiler_params=pltpu.CompilerParams(vmem_limit_bytes=63 * 2**20),
        cost_estimate=pl.CostEstimate(
            flops=flops, bytes_accessed=projections.size * 2, transcendentals=0
        ),
        name="filter_backproject",
    )(fp_start, band_offset, band_count, view_angle, projections, footprint)
    return pl.pallas_call(
        functools.partial(exchange, n_zs, n_ang),
        out_shape=jax.ShapeDtypeStruct((BAND, voxels // n_ang), F32),
        in_specs=[vmem],
        out_specs=vmem,
        scratch_shapes=[
            pltpu.VMEM((n_ang - 1, n_zs, BAND // 2, voxels), F32),
            pltpu.VMEM((n_zs, BAND // 2, voxels), F32),
            pltpu.VMEM((n_zs - 1, BAND // 2, voxels), F32),
            pltpu.SemaphoreType.DMA((peers,)),
            pltpu.SemaphoreType.DMA((peers,)),
        ],
        compiler_params=pltpu.CompilerParams(collective_id=0, has_side_effects=True),
        name="sum_slabs",
    )(partial)


def solution(mesh):
    in_specs = (
        P(("grp", "ang", "zs"), None, None),
        P(("grp", "ang", "zs")),
        P(("grp", "ang", "zs"), None),
        P(("grp", "ang", "zs"), None),
        P(("grp", "ang", "zs")),
        P(("grp", "ang"), None, None),
    )
    out_specs = P(("grp", "zs"), "ang")
    body = functools.partial(shards, mesh.shape["zs"], mesh.shape["ang"])
    return jax.shard_map(body, mesh=mesh, in_specs=in_specs, out_specs=out_specs, check_vma=False)
```
